512 devices in a mesh: pair: 64 (over z, x_lo, core), spin: 8 (over y, x_hi).
Axes of the slice: x: 4 (x_hi: 2, x_lo: 2; x = x_hi * 2 + x_lo), y: 4, z: 16, core: 2. Of those that a mesh axis runs over, the one named last changes fastest.
Arguments:
- integrals: bfloat16 [4, 6144, 6144], P(None, 'pair'), may hold values from -6 to 6
- coef: bfloat16 [4, 6144, 384], P(None, 'pair', 'spin'), may hold values from -0.078125 to 0.078125
- live: int32 [64], replicated, may hold values from 1 to 96, 4608 in all
Outputs:
- transformed: float32 [2, 4, 768, 768], P(None, None, 'spin', 'pair')
The draws below stay inside these ranges and needn't reach their ends.
Inputs may be any that keep to these rules, and one draw needn't show every extreme that they name: Some pair batch has all 96 functions live.
All inputs are finite; a program needn't handle non-finite values.
Results may differ from the reference program's by a relative error of at most 0.0029.
Values may be sent and summed in bfloat16 or wider, within the bound.
No kernel may reach another device: no remote copies, remote signals or barrier semaphores. Data moves between devices by JAX's collectives and lax.ppermute only.
A program may use at most 64 MiB of HBM per device.

```python
import math
import jax
import jax.numpy as jnp
import numpy as np
from jax import lax

NAO = 6144
NKP = 384
PQ = 4
NSP = 768
S_DEV = 96
N_PAIR = 64
N_SPIN = 8


def block_levels(stream_key, shape, split, least, top_value):
    gain, own = 1.0, jax.random.fold_in(stream_key, 6)
    for dim, blocks in split:
        heights = jnp.exp(jax.random.uniform(jax.random.fold_in(own, dim), (blocks,), jnp.float32, least / len(split), top_value / len(split)))
        gain = gain * jnp.repeat(heights, shape[dim] // blocks).reshape([-1 if axis == dim else 1 for axis in range(len(shape))])
    return gain


def profile(count, total, limit, skew):
    portions = [(1 << 20) // math.isqrt(standing ** skew) + 1 for standing in range(2, count + 1)]
    rest, counts = total - limit - (count - 1), [1] * (count - 1)
    while rest > 0:
        free = [i for i in range(count - 1) if counts[i] < limit]
        pool, budget = sum([portions[i] for i in free]), rest
        for i in free:
            extra = min(limit - counts[i], max(1, budget * portions[i] // pool), rest)
            counts[i] = counts[i] + extra
            rest = rest - extra
    return np.array([limit] + counts)


def uneven(own_key, amount, total, reach, slope):
    if amount == 2:
        one = jax.random.randint(own_key, (), max(1, total - reach), min(reach, total - 1) + 1)
        return jnp.stack([one, total - one])
    tallies = jnp.asarray(profile(amount, total, reach, slope), jnp.int32)
    pairs = (amount - 1) // 2
    donor, receiver = tallies[1:1 + 2 * pairs:2], tallies[2:2 + 2 * pairs:2]
    room = jnp.minimum(donor - 1, reach - receiver)
    passed = jax.random.randint(jax.random.fold_in(own_key, 1), (pairs,), 0, 1 << 20) % (room + 1)
    tallies = tallies.at[1:1 + 2 * pairs:2].set(donor - passed).at[2:2 + 2 * pairs:2].set(receiver + passed)
    return tallies[jax.random.permutation(jax.random.fold_in(own_key, 2), amount)]


def noise(key, shape, spread, reach, pieces=(), kind=jnp.bfloat16):
    entries = spread * jax.random.normal(key, shape, jnp.float32)
    if pieces:
        entries = entries * block_levels(key, shape, pieces, -0.22, 0.18)
    return jnp.clip(entries, -reach, reach).astype(kind)


def setup_inputs(seed: int = 0) -> dict:
    key_of = jax.random.split(jax.random.key(seed), 4)
    integrals = noise(key_of[0], (PQ, NAO, NAO), 1.0, 6.0, ((1, 64),))
    coef = noise(key_of[1], (4, NAO, NKP), NAO ** -0.5, 0.078125, ((1, 64), (2, 8)))
    live = uneven(key_of[2], N_PAIR, N_PAIR * S_DEV * 3 // 4, S_DEV, 2).astype(jnp.int32)
    return dict(integrals=integrals, coef=coef, live=live)


def full_coef(coef):
    bar = jnp.stack([-coef[2], coef[3], coef[0], -coef[1]])
    unbarred = coef.reshape(4, NAO, N_SPIN, NKP // N_SPIN)
    barred = bar.reshape(4, NAO, N_SPIN, NKP // N_SPIN)
    return jnp.concatenate([unbarred, barred], axis=3).reshape(4, NAO, NSP)


def reference(integrals, coef, live):
    index = jnp.arange(NAO, dtype=jnp.int32)
    keep = (index % S_DEV) < live[index // S_DEV]
    masked = jnp.where(keep[None, :, None], integrals, jnp.zeros((), jnp.bfloat16))
    full = full_coef(coef)
    left = full.transpose(0, 2, 1).reshape(4 * NSP, NAO)
    half = lax.dot_general(left, masked, (((1,), (2,)), ((), ())), preferred_element_type=jnp.float32)
    half = half.astype(jnp.bfloat16).reshape(4, NSP, PQ, NAO)
    columns = half.transpose(0, 3, 1, 2).reshape(4 * NAO, NSP * PQ)
    w_real = full.reshape(4 * NAO, NSP)
    w_imag = jnp.stack([full[1], -full[0], full[3], -full[2]]).reshape(4 * NAO, NSP)
    dims = (((0,), (0,)), ((), ()))
    k_real = lax.dot_general(w_real, columns, dims, preferred_element_type=jnp.float32)
    k_imag = lax.dot_general(w_imag, columns, dims, preferred_element_type=jnp.float32)
    stacked = jnp.stack([k_real, k_imag]).reshape(2, NSP, NSP, PQ)
    return stacked.transpose(0, 3, 2, 1)
```

```python
import jax
import jax.numpy as jnp
import numpy as np
from jax import lax
from jax.experimental import pallas as pl
from jax.experimental.pallas import tpu as pltpu
from jax.sharding import PartitionSpec as P

S, K, PQ, PLANES, Q, SPIN = 96, 48, 4, 16, 4, 8
J = K // Q
PLANE = Q * S
CK = 4 * K
PACKED = CK * S // 128

NEAR = [[4 * (4 * h + l) + q for l in range(4)] for h in range(4) for q in range(Q)]
FAR = [[4 * (4 * h + l) + q for h in range(4)] for l in range(4) for q in range(Q)]
LINE = [[4 * z + q for z in range(PLANES)] for q in range(Q)]
PLANE_GROUP = [[4 * z + q for q in range(Q)] for z in range(PLANES)]


def swap(bit):
    return [(i, i ^ bit) for i in range(Q * PLANES)]


def signs():
    table = (
        ((0, 1), (1, 1), (2, 1), (3, 1)),
        ((1, 1), (0, -1), (3, 1), (2, -1)),
        ((2, -1), (3, 1), (0, 1), (1, -1)),
        ((3, 1), (2, 1), (1, -1), (0, -1)),
    )
    out = np.zeros((4, 4, J, 4, J), np.float32)
    for v, row in enumerate(table):
        for c, (source, sign) in enumerate(row):
            for j in range(J):
                out[c, v, j, source, j] = sign
    return out.reshape(CK, 4 * J)


def nt(a, b):
    return lax.dot_general(a, b, (((1,), (1,)), ((), ())), preferred_element_type=jnp.float32)


def pack_kernel(coef_ref, out_ref):
    full = coef_ref[...].reshape(CK, S)
    tail = full[PACKED:]
    side = jnp.concatenate([tail[:, 32 * i : 32 * i + 32] for i in range(3)], axis=0)
    out_ref[...] = jnp.concatenate([full[:PACKED], side], axis=1)


def unpack(block):
    side = block[:, S:]
    tail = jnp.concatenate([side[K * i : K * i + K] for i in range(3)], axis=1)
    return jnp.concatenate([block[:, :S], tail], axis=0)


def half_kernel(live_ref, own_ref, other_ref, integrals_ref, half_ref, rows_ref, total_ref, plane_ref):
    step = pl.program_id(0)
    here = lax.axis_index("pair")
    z, q = here // Q, here % Q
    x, core = q // 2, q % 2

    @pl.when(step == 0)
    def _():
        total_ref[...] = jnp.zeros_like(total_ref)

    total = total_ref[...]
    for near in range(4):
        slot = near * 4 + step
        blocks = []
        for place in range(Q):
            column = (place // 2) ^ x
            mine, theirs = own_ref[column, slot], other_ref[column, slot]
            blocks.append(unpack(jnp.where(core == place % 2, mine, theirs)))
        plane = jnp.concatenate(blocks, axis=1)

        @pl.when(z == step * 4 + near)
        def _():
            plane_ref[...] = plane

        part = integrals_ref[:, :, near * PLANE : (near + 1) * PLANE].reshape(PQ * S, PLANE)
        total = total + nt(plane, part)
    total_ref[...] = total

    @pl.when(step == 3)
    def _():
        keep = lax.broadcasted_iota(jnp.int32, (CK, S), 1) < live_ref[here]
        for pq in range(PQ):
            part = jnp.where(keep, total[:, pq * S : (pq + 1) * S], 0.0)
            row = jnp.concatenate([part[c * K : (c + 1) * K] for c in range(4)], axis=1)
            half_ref[pq * K : (pq + 1) * K, :] = row.astype(jnp.bfloat16)
        row = lax.broadcasted_iota(jnp.int32, (4 * J, CK), 0)
        component = sum((row >= J * c).astype(jnp.int32) for c in range(1, 4))
        wanted = (K - J) * component + row + J * q
        pick = (lax.broadcasted_iota(jnp.int32, (4 * J, CK), 1) == wanted).astype(jnp.bfloat16)
        rows = jnp.dot(pick, plane_ref[...], preferred_element_type=jnp.float32).astype(jnp.bfloat16)
        for e in range(SPIN):
            rows_ref[e] = rows


def term_kernel(half_ref, rows_ref, signs_ref, out_ref):
    by_component = [
        jnp.concatenate([half_ref[place, :, c * S : (c + 1) * S] for place in range(Q)], axis=1) for c in range(4)
    ]
    half = jnp.concatenate(by_component, axis=1)
    weights = []
    for e in range(SPIN):
        signed = jnp.dot(signs_ref[...], rows_ref[e], preferred_element_type=jnp.float32).astype(jnp.bfloat16)
        weights.append(jnp.concatenate([signed[c * 4 * J : (c + 1) * 4 * J] for c in range(4)], axis=1))
    term = nt(jnp.concatenate(weights, axis=0), half)
    for e in range(SPIN):
        part = term[e * 4 * J : (e + 1) * 4 * J]
        side = jnp.concatenate([part[: 2 * J, 128:], part[2 * J :, 128:]], axis=1)
        block = jnp.concatenate([part[:, :128], side], axis=0).astype(jnp.bfloat16)
        out_ref[2 * e] = block
        out_ref[2 * e + 1] = block


def sum_kernel(terms_ref, out_ref):
    total = terms_ref[0].astype(jnp.float32)
    for z in range(1, PLANES):
        total = total + terms_ref[z].astype(jnp.float32)
    side = total[4 * J :]
    full = jnp.concatenate([total[: 4 * J], jnp.concatenate([side[:, :64], side[:, 64:]], axis=0)], axis=1)
    real, imag, real_bar, imag_bar = (full[v * J : (v + 1) * J] for v in range(4))
    barred = (lax.axis_index("pair") // Q) % 2 == 1
    parts = (
        (jnp.where(barred, real_bar, real), jnp.where(barred, real, -real_bar)),
        (jnp.where(barred, imag_bar, imag), jnp.where(barred, -imag, imag_bar)),
    )
    for t, (unbarred, partner) in enumerate(parts):
        for pq in range(PQ):
            columns = slice(pq * K, (pq + 1) * K)
            out_ref[t, :, pq, :] = jnp.concatenate([unbarred[:, columns], partner[:, columns]], axis=1)


def shards(integrals, coef, live):
    bf16 = jnp.bfloat16
    vmem = pl.BlockSpec(memory_space=pltpu.VMEM)
    limit = pltpu.CompilerParams(vmem_limit_bytes=48 * 1024 * 1024)
    packed = pl.pallas_call(
        pack_kernel,
        out_shape=jax.ShapeDtypeStruct((PACKED, 128), bf16),
        in_specs=[vmem],
        out_specs=vmem,
        compiler_params=limit,
    )(coef.transpose(0, 2, 1))
    line = lax.all_gather(packed, "pair", axis_index_groups=FAR, tiled=True)
    line = lax.all_gather(line, "pair", axis_index_groups=NEAR, tiled=True)
    own = jnp.concatenate([line, lax.ppermute(line, "pair", swap(2))])
    other = lax.ppermute(own, "pair", swap(1))
    half, rows = pl.pallas_call(
        half_kernel,
        grid=(4,),
        out_shape=(
            jax.ShapeDtypeStruct((PQ * K, 4 * S), bf16),
            jax.ShapeDtypeStruct((SPIN, 4 * J, PLANE), bf16),
        ),
        in_specs=[
            pl.BlockSpec(memory_space=pltpu.SMEM),
            vmem,
            vmem,
            pl.BlockSpec((PQ, S, 4 * PLANE), lambda i: (0, 0, i)),
        ],
        out_specs=(vmem, vmem),
        scratch_shapes=[pltpu.VMEM((CK, PQ * S), jnp.float32), pltpu.VMEM((CK, PLANE), bf16)],
        compiler_params=limit,
    )(live, own.reshape(2, PLANES, PACKED, 128), other.reshape(2, PLANES, PACKED, 128), integrals)
    rows = lax.all_to_all(rows, "spin", 0, 0)
    halves = lax.all_gather(half, "pair", axis_index_groups=PLANE_GROUP)
    terms = pl.pallas_call(
        term_kernel,
        out_shape=jax.ShapeDtypeStruct((PLANES, 72, 128), bf16),
        in_specs=[vmem] * 3,
        out_specs=vmem,
        compiler_params=limit,
    )(halves, rows, jnp.asarray(signs(), bf16))
    terms = lax.all_to_all(terms, "pair", 0, 0, axis_index_groups=LINE)
    out = pl.pallas_call(
        sum_kernel,
        out_shape=jax.ShapeDtypeStruct((2, J, PQ, 2 * K), jnp.float32),
        in_specs=[vmem],
        out_specs=vmem,
        compiler_params=limit,
    )(terms)
    return out.transpose(0, 2, 3, 1)


def solution(mesh):
    placed = (P(None, "pair", None), P(None, "pair", "spin"), P())
    return jax.shard_map(
        shards, mesh=mesh, in_specs=placed, out_specs=P(None, None, "spin", "pair"), check_vma=False
    )
```

```python
import jax
import jax.numpy as jnp
import numpy as np
from jax import lax
from jax.experimental import pallas as pl
from jax.experimental.pallas import tpu as pltpu
from jax.sharding import PartitionSpec as P

S, K, PQ, PLANES, Q, SPIN = 96, 48, 4, 16, 4, 8
J = K // Q
PLANE = Q * S
CK = 4 * K
PACKED = CK * S // 128

FOLD = [0, 1, 3, 2]
NEAR = [[4 * (4 * h + l) + q for l in FOLD] for h in range(4) for q in range(Q)]
FAR = [[4 * (4 * h + l) + q for h in range(4)] for l in range(4) for q in range(Q)]
LINE = [[4 * z + q for z in range(PLANES)] for q in range(Q)]
CHIP = [[2 * i, 2 * i + 1] for i in range(Q * PLANES // 2)]


def swap(bit):
    return [(i, i ^ bit) for i in range(Q * PLANES)]


def signs():
    table = (
        ((0, 1), (1, 1), (2, 1), (3, 1)),
        ((1, 1), (0, -1), (3, 1), (2, -1)),
        ((2, -1), (3, 1), (0, 1), (1, -1)),
        ((3, 1), (2, 1), (1, -1), (0, -1)),
    )
    out = np.zeros((4, 4, J, 4, J), np.float32)
    for v, row in enumerate(table):
        for c, (source, sign) in enumerate(row):
            for j in range(J):
                out[c, v, j, source, j] = sign
    return out.reshape(CK, 4 * J)


def nt(a, b):
    return lax.dot_general(a, b, (((1,), (1,)), ((), ())), preferred_element_type=jnp.float32)


def turn(x, lanes):
    return x if lanes == 0 else jnp.concatenate([x[:, 128 - lanes :], x[:, : 128 - lanes]], axis=1)


def pack_kernel(coef_ref, out_ref):
    q = lax.axis_index("pair") % Q
    full = coef_ref[...].reshape(CK, S)
    tail = full[PACKED:]
    side = jnp.concatenate([tail[:, 32 * i : 32 * i + 32] for i in range(3)], axis=0)
    packed = jnp.concatenate([full[:PACKED], side], axis=1)
    turned = packed
    for place in range(1, Q):
        turned = jnp.where(q == place, turn(packed, S * place % 128), turned)
    out_ref[...] = turned


def plane_of(blocks, lane):
    p0, p1, p2, p3 = blocks
    main = [jnp.where(lane < 96, p0, p1), jnp.where(lane < 64, p1, p2), jnp.where(lane < 32, p2, p3)]
    side = jnp.where(lane < 32, p3, jnp.where(lane < 64, p2, jnp.where(lane < 96, p1, p0)))
    turned = [turn(side[K * i : K * i + K], 32 * (i + 1)) for i in range(3)]
    low = lane[:K]
    tail = [
        jnp.where((low >= 32) & (low < 64), turned[(t + 1) % 3], jnp.where((low >= 64) & (low < 96), turned[(t + 2) % 3], turned[t]))
        for t in range(3)
    ]
    return jnp.concatenate([jnp.concatenate(main, axis=1), jnp.concatenate(tail, axis=1)], axis=0)


def half_kernel(live_ref, own_ref, other_ref, integrals_ref, half_ref):
    here = lax.axis_index("pair")
    x, core = here % Q // 2, here % 2
    lane = lax.broadcasted_iota(jnp.int32, (PACKED, 128), 1)
    total = None
    for h in range(4):
        planes = []
        for l in range(4):
            slot = FOLD.index(l) * 4 + h
            blocks = []
            for place in range(Q):
                column = (place // 2) ^ x
                blocks.append(jnp.where(core == place % 2, own_ref[column, slot], other_ref[column, slot]))
            planes.append(plane_of(blocks, lane))
        part = integrals_ref[:, :, h * 4 * PLANE : (h + 1) * 4 * PLANE].reshape(PQ * S, 4 * PLANE)
        term = nt(jnp.concatenate(planes, axis=1), part)
        total = term if total is None else total + term
    keep = lax.broadcasted_iota(jnp.int32, (CK, S), 1) < live_ref[here]
    for pq in range(PQ):
        part = jnp.where(keep, total[:, pq * S : (pq + 1) * S], 0.0)
        row = jnp.concatenate([part[c * K : (c + 1) * K] for c in range(4)], axis=1)
        half_ref[pq * K : (pq + 1) * K, :] = row.astype(jnp.bfloat16)


def rows_kernel(coef_ref, out_ref):
    core = lax.axis_index("pair") % 2
    row = lax.broadcasted_iota(jnp.int32, (8 * J, CK), 0)
    x = (row >= 4 * J).astype(jnp.int32)
    row = row - 4 * J * x
    component = sum((row >= J * c).astype(jnp.int32) for c in range(1, 4))
    wanted = (K - J) * component + row + J * (2 * x + core)
    pick = (lax.broadcasted_iota(jnp.int32, (8 * J, CK), 1) == wanted).astype(jnp.bfloat16)
    picked = [jnp.dot(pick, coef_ref[c], preferred_element_type=jnp.float32) for c in range(2)]
    rows = jnp.concatenate(picked, axis=1).astype(jnp.bfloat16)
    for e in range(SPIN):
        out_ref[e] = rows


def term_kernel(half_ref, rows_ref, signs_ref, own_ref, other_ref):
    x = lax.axis_index("pair") % Q // 2
    half = [jnp.concatenate([half_ref[core, :, c * S : (c + 1) * S] for core in range(2)], axis=1) for c in range(4)]
    terms = []
    for column in range(2):
        signed = [
            jnp.dot(signs_ref[...], rows_ref[e, 4 * J * column : 4 * J * (column + 1)], preferred_element_type=jnp.float32)
            for e in range(SPIN)
        ]
        term = None
        for c in range(4):
            weights = jnp.concatenate([part[4 * J * c : 4 * J * (c + 1)] for part in signed], axis=0)
            more = nt(weights.astype(jnp.bfloat16), half[c])
            term = more if term is None else term + more
        terms.append(term)
    own = jnp.where(x == 0, terms[0], terms[1])
    other = jnp.where(x == 0, terms[1], terms[0])
    for term, ref in ((own, own_ref), (other, other_ref)):
        for e in range(SPIN):
            part = term[e * 4 * J : (e + 1) * 4 * J]
            side = jnp.concatenate([part[: 2 * J, 128:], part[2 * J :, 128:]], axis=1)
            ref[e] = jnp.concatenate([part[:, :128], side], axis=0).astype(ref.dtype)


def join_kernel(own_ref, other_ref, out_ref):
    for e in range(SPIN):
        block = (own_ref[e] + other_ref[e].astype(jnp.float32)).astype(jnp.bfloat16)
        out_ref[2 * e] = block
        out_ref[2 * e + 1] = block


def sum_kernel(terms_ref, out_ref):
    total = terms_ref[0].astype(jnp.float32)
    for z in range(1, PLANES):
        total = total + terms_ref[z].astype(jnp.float32)
    side = total[4 * J :]
    full = jnp.concatenate([total[: 4 * J], jnp.concatenate([side[:, :64], side[:, 64:]], axis=0)], axis=1)
    real, imag, real_bar, imag_bar = (full[v * J : (v + 1) * J] for v in range(4))
    barred = (lax.axis_index("pair") // Q) % 2 == 1
    parts = (
        (jnp.where(barred, real_bar, real), jnp.where(barred, real, -real_bar)),
        (jnp.where(barred, imag_bar, imag), jnp.where(barred, -imag, imag_bar)),
    )
    for t, (unbarred, partner) in enumerate(parts):
        for pq in range(PQ):
            columns = slice(pq * K, (pq + 1) * K)
            out_ref[t, :, pq, :] = jnp.concatenate([unbarred[:, columns], partner[:, columns]], axis=1)


def call(kernel, out_shape, in_specs=None, mib=16):
    vmem = pl.BlockSpec(memory_space=pltpu.VMEM)

    def run(*args):
        return pl.pallas_call(
            kernel,
            out_shape=out_shape,
            in_specs=in_specs or [vmem] * len(args),
            out_specs=jax.tree.map(lambda _: vmem, out_shape),
            compiler_params=pltpu.CompilerParams(vmem_limit_bytes=mib * 1024 * 1024),
        )(*args)

    return run


def shards(integrals, coef, live):
    bf16 = jnp.bfloat16
    shape = jax.ShapeDtypeStruct
    vmem = pl.BlockSpec(memory_space=pltpu.VMEM)
    coef = coef.transpose(0, 2, 1)
    packed = call(pack_kernel, shape((PACKED, 128), bf16))(coef)
    line = lax.all_gather(packed, "pair", axis_index_groups=FAR, tiled=True)
    line = lax.all_gather(line, "pair", axis_index_groups=NEAR, tiled=True)
    line, coef = lax.optimization_barrier((line, coef))
    own = jnp.concatenate([line, lax.ppermute(line, "pair", swap(2))])

    pairs = lax.all_gather(coef.reshape(CK, S), "pair", axis_index_groups=CHIP)
    rows = call(rows_kernel, shape((SPIN, 8 * J, 2 * S), bf16))(pairs)
    rows = lax.all_to_all(rows, "spin", 0, 0)

    other = lax.ppermute(own, "pair", swap(1))
    half = call(
        half_kernel,
        shape((PQ * K, 4 * S), bf16),
        [pl.BlockSpec(memory_space=pltpu.SMEM), vmem, vmem, vmem],
        24,
    )(live, own.reshape(2, PLANES, PACKED, 128), other.reshape(2, PLANES, PACKED, 128), integrals)
    halves = lax.all_gather(half, "pair", axis_index_groups=CHIP)
    keep, give = call(
        term_kernel,
        (shape((SPIN, 72, 128), jnp.float32), shape((SPIN, 72, 128), bf16)),
    )(halves, rows, jnp.asarray(signs(), bf16))
    terms = call(join_kernel, shape((PLANES, 72, 128), bf16))(keep, lax.ppermute(give, "pair", swap(2)))
    terms = lax.all_to_all(terms, "pair", 0, 0, axis_index_groups=LINE)
    out = call(sum_kernel, shape((2, J, PQ, 2 * K), jnp.float32))(terms)
    return out.transpose(0, 2, 3, 1)


def solution(mesh):
    placed = (P(None, "pair", None), P(None, "pair", "spin"), P())
    return jax.shard_map(
        shards, mesh=mesh, in_specs=placed, out_specs=P(None, None, "spin", "pair"), check_vma=False
    )
```

```python
import jax
import jax.numpy as jnp
import numpy as np
from jax import lax
from jax.experimental import pallas as pl
from jax.experimental.pallas import tpu as pltpu
from jax.sharding import PartitionSpec as P

S, K, PQ, PLANES, Q, SPIN = 96, 48, 4, 16, 4, 8
J = K // Q
PLANE = Q * S
CK = 4 * K
PACKED = CK * S // 128

FOLD = [0, 1, 3, 2]
NEAR = [[4 * (4 * h + l) + q for l in FOLD] for h in range(4) for q in range(Q)]
FAR = [[4 * (4 * h + l) + q for h in range(4)] for l in range(4) for q in range(Q)]
LINE = [[4 * z + q for z in range(PLANES)] for q in range(Q)]
CHIP = [[2 * i, 2 * i + 1] for i in range(Q * PLANES // 2)]
ACROSS = [[4 * z + c, 4 * z + 2 + c] for z in range(PLANES) for c in range(2)]
ROWS = [[SPIN * (2 * i + c) + 2 * y + x for c in range(2) for y in range(4)] for i in range(Q * PLANES // 2) for x in range(2)]


def swap(bit, size=Q * PLANES):
    return [(i, i ^ bit) for i in range(size)]


def signs():
    table = (
        ((0, 1), (1, 1), (2, 1), (3, 1)),
        ((1, 1), (0, -1), (3, 1), (2, -1)),
        ((2, -1), (3, 1), (0, 1), (1, -1)),
        ((3, 1), (2, 1), (1, -1), (0, -1)),
    )
    out = np.zeros((4, 4, J, 4, J), np.float32)
    for v, row in enumerate(table):
        for c, (source, sign) in enumerate(row):
            for j in range(J):
                out[c, v, j, source, j] = sign
    return out.reshape(CK, 4 * J)


def nt(a, b):
    return lax.dot_general(a, b, (((1,), (1,)), ((), ())), preferred_element_type=jnp.float32)


def turn(x, lanes):
    return x if lanes == 0 else jnp.concatenate([x[:, 128 - lanes :], x[:, : 128 - lanes]], axis=1)


def pack_kernel(coef_ref, out_ref, rows_ref):
    q = lax.axis_index("pair") % Q
    full = coef_ref[...].reshape(CK, S)
    tail = full[PACKED:]
    side = jnp.concatenate([tail[:, 32 * i : 32 * i + 32] for i in range(3)], axis=0)
    packed = jnp.concatenate([full[:PACKED], side], axis=1)
    turned = packed
    for place in range(1, Q):
        turned = jnp.where(q == place, turn(packed, S * place % 128), turned)
    out_ref[...] = turned
    row = lax.broadcasted_iota(jnp.int32, (CK, CK), 0)
    core = (row >= 8 * J).astype(jnp.int32)
    row = row - 8 * J * core
    x = (row >= 4 * J).astype(jnp.int32)
    row = row - 4 * J * x
    component = sum((row >= J * c).astype(jnp.int32) for c in range(1, 4))
    wanted = (K - J) * component + row + J * (2 * x + core)
    pick = (lax.broadcasted_iota(jnp.int32, (CK, CK), 1) == wanted).astype(jnp.bfloat16)
    rows_ref[...] = jnp.dot(pick, full, preferred_element_type=jnp.float32).astype(jnp.bfloat16)


def plane_of(blocks, lane):
    p0, p1, p2, p3 = blocks
    main = [jnp.where(lane < 96, p0, p1), jnp.where(lane < 64, p1, p2), jnp.where(lane < 32, p2, p3)]
    side = jnp.where(lane < 32, p3, jnp.where(lane < 64, p2, jnp.where(lane < 96, p1, p0)))
    turned = [turn(side[K * i : K * i + K], 32 * (i + 1)) for i in range(3)]
    low = lane[:K]
    tail = [
        jnp.where((low >= 32) & (low < 64), turned[(t + 1) % 3], jnp.where((low >= 64) & (low < 96), turned[(t + 2) % 3], turned[t]))
        for t in range(3)
    ]
    return jnp.concatenate([jnp.concatenate(main, axis=1), jnp.concatenate(tail, axis=1)], axis=0)


def half_kernel(live_ref, own_ref, other_ref, integrals_ref, half_ref, part_ref, arrived):
    copies = []
    for h in range(4):
        columns = integrals_ref.at[:, :, pl.ds(h * 4 * PLANE, 4 * PLANE)]
        copies.append(pltpu.make_async_copy(columns, part_ref.at[h], arrived.at[h]))
        copies[h].start()
    here = lax.axis_index("pair")
    x, core = here % Q // 2, here % 2
    lane = lax.broadcasted_iota(jnp.int32, (PACKED, 128), 1)
    total = None
    for h in range(4):
        planes = []
        for l in range(4):
            slot = FOLD.index(l) * 4 + h
            blocks = []
            for place in range(Q):
                column = (place // 2) ^ x
                blocks.append(jnp.where(core == place % 2, own_ref[column, slot], other_ref[column, slot]))
            planes.append(plane_of(blocks, lane))
        copies[h].wait()
        term = nt(jnp.concatenate(planes, axis=1), part_ref[h].reshape(PQ * S, 4 * PLANE))
        total = term if total is None else total + term
    keep = lax.broadcasted_iota(jnp.int32, (CK, S), 1) < live_ref[here]
    for pq in range(PQ):
        part = jnp.where(keep, total[:, pq * S : (pq + 1) * S], 0.0)
        row = jnp.concatenate([part[c * K : (c + 1) * K] for c in range(4)], axis=1)
        half_ref[pq * K : (pq + 1) * K, :] = row.astype(jnp.bfloat16)


def rows_kernel(own_ref, other_ref, out_ref):
    for place, ref in enumerate((own_ref, other_ref)):
        for core in range(2):
            rows = ref[8 * J * core : 8 * J * (core + 1)]
            for y in range(4):
                out_ref[4 * core + y, place] = rows


def term_kernel(half_ref, rows_ref, signs_ref, keep_ref, give_ref):
    x = lax.axis_index("pair") % Q // 2
    side = lax.axis_index("spin") % 2
    half = [jnp.concatenate([half_ref[core, :, c * S : (c + 1) * S] for core in range(2)], axis=1) for c in range(4)]
    for column, ref in ((x, keep_ref), (x ^ 1, give_ref)):
        signed = []
        for e in range(SPIN):
            rows = jnp.concatenate([rows_ref[4 * core + e // 2, (e % 2) ^ side, column] for core in range(2)], axis=1)
            signed.append(jnp.dot(signs_ref[...], rows, preferred_element_type=jnp.float32).astype(jnp.bfloat16))
        term = None
        for c in range(4):
            more = nt(jnp.concatenate([part[4 * J * c : 4 * J * (c + 1)] for part in signed], axis=0), half[c])
            term = more if term is None else term + more
        for e in range(SPIN):
            part = term[e * 4 * J : (e + 1) * 4 * J]
            tail = jnp.concatenate([part[: 2 * J, 128:], part[2 * J :, 128:]], axis=1)
            ref[e] = jnp.concatenate([part[:, :128], tail], axis=0).astype(ref.dtype)


def join_kernel(keep_ref, given_ref, out_ref):
    partner = 1 - lax.axis_index("pair") % Q // 2
    for e in range(SPIN):
        block = (keep_ref[e] + given_ref[partner, e].astype(jnp.float32)).astype(jnp.bfloat16)
        out_ref[2 * e] = block
        out_ref[2 * e + 1] = block


def sum_kernel(terms_ref, out_ref):
    total = terms_ref[0].astype(jnp.float32)
    for z in range(1, PLANES):
        total = total + terms_ref[z].astype(jnp.float32)
    side = total[4 * J :]
    full = jnp.concatenate([total[: 4 * J], jnp.concatenate([side[:, :64], side[:, 64:]], axis=0)], axis=1)
    real, imag, real_bar, imag_bar = (full[v * J : (v + 1) * J] for v in range(4))
    barred = (lax.axis_index("pair") // Q) % 2 == 1
    parts = (
        (jnp.where(barred, real_bar, real), jnp.where(barred, real, -real_bar)),
        (jnp.where(barred, imag_bar, imag), jnp.where(barred, -imag, imag_bar)),
    )
    for t, (unbarred, partner) in enumerate(parts):
        for pq in range(PQ):
            columns = slice(pq * K, (pq + 1) * K)
            out_ref[t, :, pq, :] = jnp.concatenate([unbarred[:, columns], partner[:, columns]], axis=1)


def call(kernel, out_shape, in_specs=None, mib=16, **more):
    vmem = pl.BlockSpec(memory_space=pltpu.VMEM)

    def run(*args):
        return pl.pallas_call(
            kernel,
            out_shape=out_shape,
            in_specs=in_specs or [vmem] * len(args),
            out_specs=jax.tree.map(lambda _: vmem, out_shape),
            compiler_params=pltpu.CompilerParams(vmem_limit_bytes=mib * 1024 * 1024),
            **more,
        )(*args)

    return run


def shards(integrals, coef, live):
    bf16 = jnp.bfloat16
    shape = jax.ShapeDtypeStruct
    vmem = pl.BlockSpec(memory_space=pltpu.VMEM)
    coef = coef.transpose(0, 2, 1)
    packed, rows = call(pack_kernel, (shape((PACKED, 128), bf16), shape((CK, S), bf16)))(coef)
    line = lax.all_gather(packed, "pair", axis_index_groups=FAR, tiled=True)
    line = lax.all_gather(line, "pair", axis_index_groups=NEAR, tiled=True)
    line, rows = lax.optimization_barrier((line, rows))
    column = lax.ppermute(line, "pair", swap(2))
    rows = call(rows_kernel, shape((8, 2, 8 * J, S), bf16))(rows, lax.ppermute(rows, "spin", swap(1, SPIN)))
    column, rows = lax.optimization_barrier((column, rows))
    rows = lax.all_to_all(rows, ("pair", "spin"), 0, 0, axis_index_groups=ROWS).reshape(8, 2, 2, 4 * J, S)

    own = jnp.concatenate([line, column])
    other = lax.ppermute(own, "pair", swap(1))
    half = call(
        half_kernel,
        shape((PQ * K, 4 * S), bf16),
        [pl.BlockSpec(memory_space=pltpu.SMEM), vmem, vmem, pl.BlockSpec(memory_space=pltpu.HBM)],
        50,
        scratch_shapes=[pltpu.VMEM((4, PQ, S, 4 * PLANE), bf16), pltpu.SemaphoreType.DMA((4,))],
    )(live, own.reshape(2, PLANES, PACKED, 128), other.reshape(2, PLANES, PACKED, 128), integrals)
    halves = lax.all_gather(half, "pair", axis_index_groups=CHIP)
    sign = jnp.asarray(signs(), bf16)
    keep, give = call(term_kernel, (shape((SPIN, 72, 128), jnp.float32), shape((SPIN, 72, 128), bf16)))(halves, rows, sign)
    given = lax.all_gather(give, "pair", axis_index_groups=ACROSS)
    terms = call(join_kernel, shape((PLANES, 72, 128), bf16))(keep, given)
    terms = lax.all_to_all(terms, "pair", 0, 0, axis_index_groups=LINE)
    out = call(sum_kernel, shape((2, J, PQ, 2 * K), jnp.float32))(terms)
    return out.transpose(0, 2, 3, 1)


def solution(mesh):
    placed = (P(None, "pair", None), P(None, "pair", "spin"), P())
    return jax.shard_map(
        shards, mesh=mesh, in_specs=placed, out_specs=P(None, None, "spin", "pair"), check_vma=False
    )
```

```python
import jax
import jax.numpy as jnp
import numpy as np
from jax import lax
from jax.experimental import pallas as pl
from jax.experimental.pallas import tpu as pltpu
from jax.sharding import PartitionSpec as P

S, K, PQ, PLANES, Q, SPIN = 96, 48, 4, 16, 4, 8
J = K // Q
PLANE = Q * S
CK = 4 * K
PACKED = CK * S // 128

FOLD = [0, 1, 3, 2]
NEAR = [[4 * (4 * h + l) + q for l in FOLD] for h in range(4) for q in range(Q)]
FAR = [[4 * (4 * h + l) + q for h in range(4)] for l in range(4) for q in range(Q)]
LINE = [[4 * z + q for z in range(PLANES)] for q in range(Q)]
CHIP = [[2 * i, 2 * i + 1] for i in range(Q * PLANES // 2)]
ACROSS = [[4 * z + c, 4 * z + 2 + c] for z in range(PLANES) for c in range(2)]
ROWS = [[SPIN * (2 * i + c) + 2 * y + x for c in range(2) for y in range(4)] for i in range(Q * PLANES // 2) for x in range(2)]


def swap(bit, size=Q * PLANES):
    return [(i, i ^ bit) for i in range(size)]


def signs():
    table = (
        ((0, 1), (1, 1), (2, 1), (3, 1)),
        ((1, 1), (0, -1), (3, 1), (2, -1)),
        ((2, -1), (3, 1), (0, 1), (1, -1)),
        ((3, 1), (2, 1), (1, -1), (0, -1)),
    )
    out = np.zeros((4, 4, J, 4, J), np.float32)
    for v, row in enumerate(table):
        for c, (source, sign) in enumerate(row):
            for j in range(J):
                out[c, v, j, source, j] = sign
    return out.reshape(CK, 4 * J)


def nt(a, b):
    return lax.dot_general(a, b, (((1,), (1,)), ((), ())), preferred_element_type=jnp.float32)


def turn(x, lanes):
    return x if lanes == 0 else jnp.concatenate([x[:, 128 - lanes :], x[:, : 128 - lanes]], axis=1)


def pack_kernel(coef_ref, out_ref, rows_ref):
    q = lax.axis_index("pair") % Q
    full = coef_ref[...].reshape(CK, S)
    tail = full[PACKED:]
    side = jnp.concatenate([tail[:, 32 * i : 32 * i + 32] for i in range(3)], axis=0)
    packed = jnp.concatenate([full[:PACKED], side], axis=1)
    turned = packed
    for place in range(1, Q):
        turned = jnp.where(q == place, turn(packed, S * place % 128), turned)
    out_ref[...] = turned
    row = lax.broadcasted_iota(jnp.int32, (CK, CK), 0)
    core = (row >= 8 * J).astype(jnp.int32)
    row = row - 8 * J * core
    x = (row >= 4 * J).astype(jnp.int32)
    row = row - 4 * J * x
    component = sum((row >= J * c).astype(jnp.int32) for c in range(1, 4))
    wanted = (K - J) * component + row + J * (2 * x + core)
    pick = (lax.broadcasted_iota(jnp.int32, (CK, CK), 1) == wanted).astype(jnp.bfloat16)
    rows = jnp.dot(pick, full, preferred_element_type=jnp.float32).astype(jnp.bfloat16)
    for group in range(8):
        rows_ref[group] = rows[8 * J * (group // 4) : 8 * J * (group // 4 + 1)]


def plane_of(blocks, lane):
    p0, p1, p2, p3 = blocks
    main = [jnp.where(lane < 96, p0, p1), jnp.where(lane < 64, p1, p2), jnp.where(lane < 32, p2, p3)]
    side = jnp.where(lane < 32, p3, jnp.where(lane < 64, p2, jnp.where(lane < 96, p1, p0)))
    turned = [turn(side[K * i : K * i + K], 32 * (i + 1)) for i in range(3)]
    low = lane[:K]
    tail = [
        jnp.where((low >= 32) & (low < 64), turned[(t + 1) % 3], jnp.where((low >= 64) & (low < 96), turned[(t + 2) % 3], turned[t]))
        for t in range(3)
    ]
    return jnp.concatenate([jnp.concatenate(main, axis=1), jnp.concatenate(tail, axis=1)], axis=0)


def half_kernel(live_ref, own_ref, other_ref, integrals_ref, half_ref, part_ref, arrived):
    copies = []
    for h in range(4):
        columns = integrals_ref.at[:, :, pl.ds(h * 4 * PLANE, 4 * PLANE)]
        copies.append(pltpu.make_async_copy(columns, part_ref.at[h], arrived.at[h]))
        copies[h].start()
    here = lax.axis_index("pair")
    x, core = here % Q // 2, here % 2
    lane = lax.broadcasted_iota(jnp.int32, (PACKED, 128), 1)
    total = None
    for h in range(4):
        planes = []
        for l in range(4):
            slot = FOLD.index(l) * 4 + h
            blocks = []
            for place in range(Q):
                column = (place // 2) ^ x
                blocks.append(jnp.where(core == place % 2, own_ref[column, slot], other_ref[column, slot]))
            planes.append(plane_of(blocks, lane))
        copies[h].wait()
        term = nt(jnp.concatenate(planes, axis=1), part_ref[h].reshape(PQ * S, 4 * PLANE))
        total = term if total is None else total + term
    keep = lax.broadcasted_iota(jnp.int32, (CK, S), 1) < live_ref[here]
    for pq in range(PQ):
        part = jnp.where(keep, total[:, pq * S : (pq + 1) * S], 0.0)
        row = jnp.concatenate([part[c * K : (c + 1) * K] for c in range(4)], axis=1)
        half_ref[pq * K : (pq + 1) * K, :] = row.astype(jnp.bfloat16)


def term_kernel(half_ref, rows_ref, far_rows_ref, signs_ref, keep_ref, give_ref):
    x = lax.axis_index("pair") % Q // 2
    side = lax.axis_index("spin") % 2
    half = [jnp.concatenate([half_ref[core, :, c * S : (c + 1) * S] for core in range(2)], axis=1) for c in range(4)]
    for column, ref in ((x, keep_ref), (x ^ 1, give_ref)):
        signed = []
        for e in range(SPIN):
            groups = [4 * core + e // 2 for core in range(2)]
            rows = jnp.concatenate([jnp.where(side == e % 2, rows_ref[g, column], far_rows_ref[g, column]) for g in groups], axis=1)
            signed.append(jnp.dot(signs_ref[...], rows, preferred_element_type=jnp.float32).astype(jnp.bfloat16))
        term = None
        for c in range(4):
            more = nt(jnp.concatenate([part[4 * J * c : 4 * J * (c + 1)] for part in signed], axis=0), half[c])
            term = more if term is None else term + more
        for e in range(SPIN):
            part = term[e * 4 * J : (e + 1) * 4 * J]
            tail = jnp.concatenate([part[: 2 * J, 128:], part[2 * J :, 128:]], axis=1)
            ref[e] = jnp.concatenate([part[:, :128], tail], axis=0).astype(ref.dtype)


def join_kernel(keep_ref, given_ref, out_ref):
    partner = 1 - lax.axis_index("pair") % Q // 2
    for e in range(SPIN):
        block = (keep_ref[e] + given_ref[partner, e].astype(jnp.float32)).astype(jnp.bfloat16)
        out_ref[2 * e] = block
        out_ref[2 * e + 1] = block


def sum_kernel(terms_ref, out_ref):
    total = terms_ref[0].astype(jnp.float32)
    for z in range(1, PLANES):
        total = total + terms_ref[z].astype(jnp.float32)
    side = total[4 * J :]
    full = jnp.concatenate([total[: 4 * J], jnp.concatenate([side[:, :64], side[:, 64:]], axis=0)], axis=1)
    real, imag, real_bar, imag_bar = (full[v * J : (v + 1) * J] for v in range(4))
    barred = (lax.axis_index("pair") // Q) % 2 == 1
    parts = (
        (jnp.where(barred, real_bar, real), jnp.where(barred, real, -real_bar)),
        (jnp.where(barred, imag_bar, imag), jnp.where(barred, -imag, imag_bar)),
    )
    for t, (unbarred, partner) in enumerate(parts):
        for pq in range(PQ):
            columns = slice(pq * K, (pq + 1) * K)
            out_ref[t, :, pq, :] = jnp.concatenate([unbarred[:, columns], partner[:, columns]], axis=1)


def call(kernel, out_shape, in_specs=None, mib=16, **more):
    vmem = pl.BlockSpec(memory_space=pltpu.VMEM)

    def run(*args):
        return pl.pallas_call(
            kernel,
            out_shape=out_shape,
            in_specs=in_specs or [vmem] * len(args),
            out_specs=jax.tree.map(lambda _: vmem, out_shape),
            compiler_params=pltpu.CompilerParams(vmem_limit_bytes=mib * 1024 * 1024),
            **more,
        )(*args)

    return run


def shards(integrals, coef, live):
    bf16 = jnp.bfloat16
    shape = jax.ShapeDtypeStruct
    vmem = pl.BlockSpec(memory_space=pltpu.VMEM)
    coef = coef.transpose(0, 2, 1)
    packed, rows = call(pack_kernel, (shape((PACKED, 128), bf16), shape((8, 8 * J, S), bf16)))(coef)
    line = lax.all_gather(packed, "pair", axis_index_groups=FAR, tiled=True)
    line = lax.all_gather(line, "pair", axis_index_groups=NEAR, tiled=True)
    line, rows = lax.optimization_barrier((line, rows))
    column = lax.ppermute(line, "pair", swap(2))
    rows = lax.all_to_all(rows, ("pair", "spin"), 0, 0, axis_index_groups=ROWS)
    column, rows = lax.optimization_barrier((column, rows))
    far_rows = lax.ppermute(rows, "spin", swap(1, SPIN))

    own = jnp.concatenate([line, column])
    other = lax.ppermute(own, "pair", swap(1))
    half = call(
        half_kernel,
        shape((PQ * K, 4 * S), bf16),
        [pl.BlockSpec(memory_space=pltpu.SMEM), vmem, vmem, pl.BlockSpec(memory_space=pltpu.HBM)],
        50,
        scratch_shapes=[pltpu.VMEM((4, PQ, S, 4 * PLANE), bf16), pltpu.SemaphoreType.DMA((4,))],
    )(live, own.reshape(2, PLANES, PACKED, 128), other.reshape(2, PLANES, PACKED, 128), integrals)
    halves = lax.all_gather(half, "pair", axis_index_groups=CHIP)
    sign = jnp.asarray(signs(), bf16)
    keep, give = call(term_kernel, (shape((SPIN, 72, 128), jnp.float32), shape((SPIN, 72, 128), bf16)))(
        halves, rows.reshape(8, 2, 4 * J, S), far_rows.reshape(8, 2, 4 * J, S), sign
    )
    given = lax.all_gather(give, "pair", axis_index_groups=ACROSS)
    terms = call(join_kernel, shape((PLANES, 72, 128), bf16))(keep, given)
    terms = lax.all_to_all(terms, "pair", 0, 0, axis_index_groups=LINE)
    out = call(sum_kernel, shape((2, J, PQ, 2 * K), jnp.float32))(terms)
    return out.transpose(0, 2, 3, 1)


def solution(mesh):
    placed = (P(None, "pair", None), P(None, "pair", "spin"), P())
    return jax.shard_map(
        shards, mesh=mesh, in_specs=placed, out_specs=P(None, None, "spin", "pair"), check_vma=False
    )
```

```python
import jax
import jax.numpy as jnp
import numpy as np
from jax import lax
from jax.experimental import pallas as pl
from jax.experimental.pallas import tpu as pltpu
from jax.sharding import PartitionSpec as P

S, K, PQ, PLANES, Q, SPIN = 96, 48, 4, 16, 4, 8
J = K // Q
PLANE = Q * S
CK = 4 * K
PACKED = CK * S // 128

FOLD = [0, 1, 3, 2]
NEAR = [[4 * (4 * h + l) + q for l in FOLD] for h in range(4) for q in range(Q)]
FAR = [[4 * (4 * h + l) + q for h in range(4)] for l in range(4) for q in range(Q)]
LINE = [[4 * z + q for z in range(PLANES)] for q in range(Q)]
CHIP = [[2 * i, 2 * i + 1] for i in range(Q * PLANES // 2)]
PLANE_PAIRS = [[8 * z + q, 8 * z + 4 + q] for z in range(PLANES // 2) for q in range(Q)]
ACROSS = [[4 * z + c, 4 * z + 2 + c] for z in range(PLANES) for c in range(2)]
ROWS = [[SPIN * (2 * i + c) + 2 * y + x for c in range(2) for y in range(4)] for i in range(Q * PLANES // 2) for x in range(2)]


def swap(bit, size=Q * PLANES):
    return [(i, i ^ bit) for i in range(size)]


def signs():
    table = (
        ((0, 1), (1, 1), (2, 1), (3, 1)),
        ((1, 1), (0, -1), (3, 1), (2, -1)),
        ((2, -1), (3, 1), (0, 1), (1, -1)),
        ((3, 1), (2, 1), (1, -1), (0, -1)),
    )
    out = np.zeros((4, 4, J, 4, J), np.float32)
    for v, row in enumerate(table):
        for c, (source, sign) in enumerate(row):
            for j in range(J):
                out[c, v, j, source, j] = sign
    return np.kron(np.eye(2, dtype=np.float32), out.reshape(CK, 4 * J))


def nt(a, b):
    return lax.dot_general(a, b, (((1,), (1,)), ((), ())), preferred_element_type=jnp.float32)


def turn(x, lanes):
    return x if lanes == 0 else jnp.concatenate([x[:, 128 - lanes :], x[:, : 128 - lanes]], axis=1)


def pack_kernel(coef_ref, out_ref, rows_ref):
    q = lax.axis_index("pair") % Q
    full = coef_ref[...].reshape(CK, S)
    tail = full[PACKED:]
    side = jnp.concatenate([tail[:, 32 * i : 32 * i + 32] for i in range(3)], axis=0)
    packed = jnp.concatenate([full[:PACKED], side], axis=1)
    turned = packed
    for place in range(1, Q):
        turned = jnp.where(q == place, turn(packed, S * place % 128), turned)
    out_ref[...] = turned
    row = lax.broadcasted_iota(jnp.int32, (CK, CK), 0)
    core = (row >= 8 * J).astype(jnp.int32)
    row = row - 8 * J * core
    x = (row >= 4 * J).astype(jnp.int32)
    row = row - 4 * J * x
    component = sum((row >= J * c).astype(jnp.int32) for c in range(1, 4))
    wanted = (K - J) * component + row + J * (2 * x + core)
    pick = (lax.broadcasted_iota(jnp.int32, (CK, CK), 1) == wanted).astype(jnp.bfloat16)
    rows = jnp.dot(pick, full, preferred_element_type=jnp.float32)
    for core in range(2):
        first, second = (rows[4 * J * i : 4 * J * (i + 1)] for i in (2 * core, 2 * core + 1))
        top = jnp.concatenate([first, second[:, :32]], axis=1)
        low = jnp.concatenate([second[: 2 * J, 32:], second[2 * J :, 32:]], axis=1)
        block = jnp.concatenate([top, low], axis=0).astype(jnp.bfloat16)
        for y in range(4):
            rows_ref[4 * core + y] = block


def plane_of(blocks, lane):
    p0, p1, p2, p3 = blocks
    main = [jnp.where(lane < 96, p0, p1), jnp.where(lane < 64, p1, p2), jnp.where(lane < 32, p2, p3)]
    side = jnp.where(lane < 32, p3, jnp.where(lane < 64, p2, jnp.where(lane < 96, p1, p0)))
    turned = [turn(side[K * i : K * i + K], 32 * (i + 1)) for i in range(3)]
    low = lane[:K]
    tail = [
        jnp.where((low >= 32) & (low < 64), turned[(t + 1) % 3], jnp.where((low >= 64) & (low < 96), turned[(t + 2) % 3], turned[t]))
        for t in range(3)
    ]
    return jnp.concatenate([jnp.concatenate(main, axis=1), jnp.concatenate(tail, axis=1)], axis=0)


def half_kernel(live_ref, own_ref, other_ref, integrals_ref, half_ref, total_ref):
    step = pl.program_id(0)
    here = lax.axis_index("pair")
    x, core = here % Q // 2, here % 2
    lane = lax.broadcasted_iota(jnp.int32, (PACKED, 128), 1)
    planes = []
    for i in range(PLANES // 2):
        slot = FOLD.index(i % 4) * 4 + 2 * step + i // 4
        blocks = []
        for place in range(Q):
            column = (place // 2) ^ x
            blocks.append(jnp.where(core == place % 2, own_ref[column, slot], other_ref[column, slot]))
        planes.append(plane_of(blocks, lane))
    term = nt(jnp.concatenate(planes, axis=1), integrals_ref[...].reshape(PQ * S, PLANES * PLANE // 2))

    @pl.when(step == 0)
    def _():
        total_ref[...] = term

    @pl.when(step == 1)
    def _():
        total = total_ref[...] + term
        keep = lax.broadcasted_iota(jnp.int32, (CK, S), 1) < live_ref[here]
        for pq in range(PQ):
            part = jnp.where(keep, total[:, pq * S : (pq + 1) * S], 0.0)
            row = jnp.concatenate([part[c * K : (c + 1) * K] for c in range(4)], axis=1)
            half_ref[pq * K : (pq + 1) * K, :] = row.astype(jnp.bfloat16)


def rows_of(block):
    block = block.astype(jnp.float32)
    low = jnp.concatenate([block[4 * J :, :64], block[4 * J :, 64:]], axis=0)
    return jnp.concatenate([block[: 4 * J, :S], jnp.concatenate([block[: 4 * J, S:], low], axis=1)], axis=0)


def term_kernel(half_ref, rows_ref, far_rows_ref, signs_ref, keep_ref, give_ref):
    x = lax.axis_index("pair") % Q // 2
    side = lax.axis_index("spin") % 2
    half = [jnp.concatenate([half_ref[core, :, c * S : (c + 1) * S] for core in range(2)], axis=1) for c in range(4)]
    signed = []
    for e in range(SPIN):
        groups = [4 * core + e // 2 for core in range(2)]
        rows = [rows_of(jnp.where(side == e % 2, rows_ref[g], far_rows_ref[g])) for g in groups]
        rows = jnp.concatenate(rows, axis=1).astype(jnp.bfloat16)
        signed.append(jnp.dot(signs_ref[...], rows, preferred_element_type=jnp.float32).astype(jnp.bfloat16))
    terms = []
    for column in range(2):
        term = None
        for c in range(4):
            at = 4 * J * (4 * column + c)
            more = nt(jnp.concatenate([part[at : at + 4 * J] for part in signed], axis=0), half[c])
            term = more if term is None else term + more
        terms.append(term)
    for term, ref in ((jnp.where(x == 0, terms[0], terms[1]), keep_ref), (jnp.where(x == 0, terms[1], terms[0]), give_ref)):
        for e in range(SPIN):
            part = term[e * 4 * J : (e + 1) * 4 * J]
            tail = jnp.concatenate([part[: 2 * J, 128:], part[2 * J :, 128:]], axis=1)
            ref[e] = jnp.concatenate([part[:, :128], tail], axis=0).astype(ref.dtype)


def join_kernel(keep_ref, given_ref, out_ref):
    partner = 1 - lax.axis_index("pair") % Q // 2
    for e in range(SPIN):
        block = keep_ref[e] + given_ref[partner, e].astype(jnp.float32)
        out_ref[2 * e] = block[:40].astype(jnp.bfloat16)
        out_ref[2 * e + 1] = block[32:].astype(jnp.bfloat16)


def sum_kernel(terms_ref, out_ref):
    total = terms_ref[0].astype(jnp.float32)
    for z in range(1, PLANES):
        total = total + terms_ref[z].astype(jnp.float32)
    out_ref[...] = total


def result_kernel(sums_ref, out_ref):
    total = jnp.concatenate([sums_ref[0], sums_ref[1, 8:]], axis=0)
    side = total[4 * J :]
    full = jnp.concatenate([total[: 4 * J], jnp.concatenate([side[:, :64], side[:, 64:]], axis=0)], axis=1)
    real, imag, real_bar, imag_bar = (full[v * J : (v + 1) * J] for v in range(4))
    barred = (lax.axis_index("pair") // Q) % 2 == 1
    parts = (
        (jnp.where(barred, real_bar, real), jnp.where(barred, real, -real_bar)),
        (jnp.where(barred, imag_bar, imag), jnp.where(barred, -imag, imag_bar)),
    )
    for t, (unbarred, partner) in enumerate(parts):
        for pq in range(PQ):
            columns = slice(pq * K, (pq + 1) * K)
            out_ref[t, :, pq, :] = jnp.concatenate([unbarred[:, columns], partner[:, columns]], axis=1)


def call(kernel, out_shape, in_specs=None, mib=16, **more):
    vmem = pl.BlockSpec(memory_space=pltpu.VMEM)

    def run(*args):
        return pl.pallas_call(
            kernel,
            out_shape=out_shape,
            in_specs=in_specs or [vmem] * len(args),
            out_specs=jax.tree.map(lambda _: vmem, out_shape),
            compiler_params=pltpu.CompilerParams(vmem_limit_bytes=mib * 1024 * 1024),
            **more,
        )(*args)

    return run


def shards(integrals, coef, live):
    bf16 = jnp.bfloat16
    shape = jax.ShapeDtypeStruct
    vmem = pl.BlockSpec(memory_space=pltpu.VMEM)
    coef = coef.transpose(0, 2, 1)
    packed, rows = call(pack_kernel, (shape((PACKED, 128), bf16), shape((8, 72, 128), bf16)))(coef)
    line = lax.all_gather(packed, "pair", axis_index_groups=FAR, tiled=True)
    line = lax.all_gather(line, "pair", axis_index_groups=NEAR, tiled=True)
    line, rows = lax.optimization_barrier((line, rows))
    column = lax.ppermute(line, "pair", swap(2))
    rows = lax.all_to_all(rows, ("pair", "spin"), 0, 0, axis_index_groups=ROWS)
    column, rows = lax.optimization_barrier((column, rows))
    far_rows = lax.ppermute(rows, "spin", swap(1, SPIN))

    own = jnp.concatenate([line, column])
    other = lax.ppermute(own, "pair", swap(1))
    half = call(
        half_kernel,
        shape((PQ * K, 4 * S), bf16),
        [pl.BlockSpec(memory_space=pltpu.SMEM), vmem, vmem, pl.BlockSpec((PQ, S, PLANES * PLANE // 2), lambda i: (0, 0, i))],
        50,
        grid=(2,),
        scratch_shapes=[pltpu.VMEM((CK, PQ * S), jnp.float32)],
    )(live, own.reshape(2, PLANES, PACKED, 128), other.reshape(2, PLANES, PACKED, 128), integrals)
    halves = lax.all_gather(half, "pair", axis_index_groups=CHIP)
    sign = jnp.asarray(signs(), bf16)
    keep, give = call(term_kernel, (shape((SPIN, 72, 128), jnp.float32), shape((SPIN, 72, 128), bf16)))(
        halves, rows, far_rows, sign
    )
    given = lax.all_gather(give, "pair", axis_index_groups=ACROSS)
    terms = call(join_kernel, shape((PLANES, 40, 128), bf16))(keep, given)
    terms = lax.all_to_all(terms, "pair", 0, 0, axis_index_groups=LINE)
    sums = call(sum_kernel, shape((40, 128), jnp.float32))(terms)
    sums = lax.all_gather(sums, "pair", axis_index_groups=PLANE_PAIRS)
    out = call(result_kernel, shape((2, J, PQ, 2 * K), jnp.float32))(sums)
    return out.transpose(0, 2, 3, 1)


def solution(mesh):
    placed = (P(None, "pair", None), P(None, "pair", "spin"), P())
    return jax.shard_map(
        shards, mesh=mesh, in_specs=placed, out_specs=P(None, None, "spin", "pair"), check_vma=False
    )
```

```python
import jax
import jax.numpy as jnp
import numpy as np
from jax import lax
from jax.experimental import pallas as pl
from jax.experimental.pallas import tpu as pltpu
from jax.sharding import PartitionSpec as P

S, K, PQ, PLANES, Q, SPIN = 96, 48, 4, 16, 4, 8
J = K // Q
PLANE = Q * S
CK = 4 * K
PACKED = CK * S // 128

FOLD = [0, 1, 3, 2]
NEAR = [[4 * (4 * h + l) + q for l in FOLD] for h in range(4) for q in range(Q)]
FAR = [[4 * (4 * h + l) + q for h in range(4)] for l in range(4) for q in range(Q)]
LINE = [[4 * z + q for z in range(PLANES)] for q in range(Q)]
CHIP = [[2 * i, 2 * i + 1] for i in range(Q * PLANES // 2)]
PLANE_PAIRS = [[8 * z + q, 8 * z + 4 + q] for z in range(PLANES // 2) for q in range(Q)]
ACROSS = [[4 * z + c, 4 * z + 2 + c] for z in range(PLANES) for c in range(2)]
ROWS = [[SPIN * (2 * i + c) + 2 * y + x for c in range(2) for y in range(4)] for i in range(Q * PLANES // 2) for x in range(2)]


def swap(bit, size=Q * PLANES):
    return [(i, i ^ bit) for i in range(size)]


def signs():
    table = (
        ((0, 1), (1, 1), (2, 1), (3, 1)),
        ((1, 1), (0, -1), (3, 1), (2, -1)),
        ((2, -1), (3, 1), (0, 1), (1, -1)),
        ((3, 1), (2, 1), (1, -1), (0, -1)),
    )
    out = np.zeros((4, 4, J, 4, J), np.float32)
    for v, row in enumerate(table):
        for c, (source, sign) in enumerate(row):
            for j in range(J):
                out[c, v, j, source, j] = sign
    return np.kron(np.eye(2, dtype=np.float32), out.reshape(CK, 4 * J))


def nt(a, b):
    return lax.dot_general(a, b, (((1,), (1,)), ((), ())), preferred_element_type=jnp.float32)


def turn(x, lanes):
    return x if lanes == 0 else jnp.concatenate([x[:, 128 - lanes :], x[:, : 128 - lanes]], axis=1)


def pack_kernel(coef_ref, out_ref, rows_ref):
    q = lax.axis_index("pair") % Q
    full = coef_ref[...].reshape(CK, S)
    tail = full[PACKED:]
    side = jnp.concatenate([tail[:, 32 * i : 32 * i + 32] for i in range(3)], axis=0)
    packed = jnp.concatenate([full[:PACKED], side], axis=1)
    turned = packed
    for place in range(1, Q):
        turned = jnp.where(q == place, turn(packed, S * place % 128), turned)
    out_ref[...] = turned
    row = lax.broadcasted_iota(jnp.int32, (CK, CK), 0)
    core = (row >= 8 * J).astype(jnp.int32)
    row = row - 8 * J * core
    x = (row >= 4 * J).astype(jnp.int32)
    row = row - 4 * J * x
    component = sum((row >= J * c).astype(jnp.int32) for c in range(1, 4))
    wanted = (K - J) * component + row + J * (2 * x + core)
    pick = (lax.broadcasted_iota(jnp.int32, (CK, CK), 1) == wanted).astype(jnp.bfloat16)
    rows = jnp.dot(pick, full, preferred_element_type=jnp.float32)
    for core in range(2):
        first, second = (rows[4 * J * i : 4 * J * (i + 1)] for i in (2 * core, 2 * core + 1))
        top = jnp.concatenate([first, second[:, :32]], axis=1)
        low = jnp.concatenate([second[: 2 * J, 32:], second[2 * J :, 32:]], axis=1)
        block = jnp.concatenate([top, low], axis=0).astype(jnp.bfloat16)
        for y in range(4):
            rows_ref[4 * core + y] = block


def plane_of(blocks, lane):
    p0, p1, p2, p3 = blocks
    main = [jnp.where(lane < 96, p0, p1), jnp.where(lane < 64, p1, p2), jnp.where(lane < 32, p2, p3)]
    side = jnp.where(lane < 32, p3, jnp.where(lane < 64, p2, jnp.where(lane < 96, p1, p0)))
    turned = [turn(side[K * i : K * i + K], 32 * (i + 1)) for i in range(3)]
    low = lane[:K]
    tail = [
        jnp.where((low >= 32) & (low < 64), turned[(t + 1) % 3], jnp.where((low >= 64) & (low < 96), turned[(t + 2) % 3], turned[t]))
        for t in range(3)
    ]
    return jnp.concatenate([jnp.concatenate(main, axis=1), jnp.concatenate(tail, axis=1)], axis=0)


def half_kernel(live_ref, own_ref, other_ref, integrals_ref, half_ref, total_ref):
    step = pl.program_id(0)
    here = lax.axis_index("pair")
    x, core = here % Q // 2, here % 2
    lane = lax.broadcasted_iota(jnp.int32, (PACKED, 128), 1)
    planes = []
    for i in range(PLANES // 2):
        slot = FOLD.index(i % 4) * 4 + 2 * step + i // 4
        blocks = []
        for place in range(Q):
            column = (place // 2) ^ x
            blocks.append(jnp.where(core == place % 2, own_ref[column, slot], other_ref[column, slot]))
        planes.append(plane_of(blocks, lane))
    term = nt(jnp.concatenate(planes, axis=1), integrals_ref[...].reshape(PQ * S, PLANES * PLANE // 2))

    @pl.when(step == 0)
    def _():
        total_ref[...] = term

    @pl.when(step == 1)
    def _():
        total = total_ref[...] + term
        keep = lax.broadcasted_iota(jnp.int32, (CK, S), 1) < live_ref[here]
        for pq in range(PQ):
            part = jnp.where(keep, total[:, pq * S : (pq + 1) * S], 0.0)
            row = jnp.concatenate([part[c * K : (c + 1) * K] for c in range(4)], axis=1)
            half_ref[pq * K : (pq + 1) * K, :] = row.astype(jnp.bfloat16)


def rows_of(block):
    block = block.astype(jnp.float32)
    low = jnp.concatenate([block[4 * J :, :64], block[4 * J :, 64:]], axis=0)
    return jnp.concatenate([block[: 4 * J, :S], jnp.concatenate([block[: 4 * J, S:], low], axis=1)], axis=0)


def term_kernel(half_ref, rows_ref, far_rows_ref, signs_ref, keep_ref, give_ref):
    x = lax.axis_index("pair") % Q // 2
    side = lax.axis_index("spin") % 2
    half = [jnp.concatenate([half_ref[core, :, c * S : (c + 1) * S] for core in range(2)], axis=1) for c in range(4)]
    signed = []
    for e in range(SPIN):
        groups = [4 * core + e // 2 for core in range(2)]
        rows = [rows_of(jnp.where(side == e % 2, rows_ref[g], far_rows_ref[g])) for g in groups]
        rows = jnp.concatenate(rows, axis=1).astype(jnp.bfloat16)
        signed.append(jnp.dot(signs_ref[...], rows, preferred_element_type=jnp.float32).astype(jnp.bfloat16))
    terms = []
    for column in range(2):
        term = None
        for c in range(4):
            at = 4 * J * (4 * column + c)
            more = nt(jnp.concatenate([part[at : at + 4 * J] for part in signed], axis=0), half[c])
            term = more if term is None else term + more
        terms.append(term)
    for term, ref in ((jnp.where(x == 0, terms[0], terms[1]), keep_ref), (jnp.where(x == 0, terms[1], terms[0]), give_ref)):
        for e in range(SPIN):
            part = term[e * 4 * J : (e + 1) * 4 * J]
            tail = jnp.concatenate([part[: 2 * J, 128:], part[2 * J :, 128:]], axis=1)
            ref[e] = jnp.concatenate([part[:, :128], tail], axis=0).astype(ref.dtype)


def join_kernel(keep_ref, given_ref, out_ref):
    partner = 1 - lax.axis_index("pair") % Q // 2
    for e in range(SPIN):
        block = keep_ref[e] + given_ref[partner, e].astype(jnp.float32)
        out_ref[2 * e] = block[:40].astype(jnp.bfloat16)
        out_ref[2 * e + 1] = block[32:].astype(jnp.bfloat16)


def sum_kernel(terms_ref, out_ref):
    total = terms_ref[0].astype(jnp.float32)
    for z in range(1, PLANES):
        total = total + terms_ref[z].astype(jnp.float32)
    out_ref[...] = total


def result_kernel(sums_ref, out_ref):
    total = jnp.concatenate([sums_ref[0], sums_ref[1, 8:]], axis=0)
    side = total[4 * J :]
    full = jnp.concatenate([total[: 4 * J], jnp.concatenate([side[:, :64], side[:, 64:]], axis=0)], axis=1)
    real, imag, real_bar, imag_bar = (full[v * J : (v + 1) * J] for v in range(4))
    barred = (lax.axis_index("pair") // Q) % 2 == 1
    parts = (
        (jnp.where(barred, real_bar, real), jnp.where(barred, real, -real_bar)),
        (jnp.where(barred, imag_bar, imag), jnp.where(barred, -imag, imag_bar)),
    )
    for t, (unbarred, partner) in enumerate(parts):
        for pq in range(PQ):
            columns = slice(pq * K, (pq + 1) * K)
            out_ref[t, :, pq, :] = jnp.concatenate([unbarred[:, columns], partner[:, columns]], axis=1)


def call(kernel, out_shape, in_specs=None, mib=16, **more):
    vmem = pl.BlockSpec(memory_space=pltpu.VMEM)

    def run(*args):
        return pl.pallas_call(
            kernel,
            out_shape=out_shape,
            in_specs=in_specs or [vmem] * len(args),
            out_specs=jax.tree.map(lambda _: vmem, out_shape),
            compiler_params=pltpu.CompilerParams(vmem_limit_bytes=mib * 1024 * 1024),
            **more,
        )(*args)

    return run


def shards(integrals, coef, live):
    bf16 = jnp.bfloat16
    shape = jax.ShapeDtypeStruct
    vmem = pl.BlockSpec(memory_space=pltpu.VMEM)
    coef = coef.transpose(0, 2, 1)
    packed, rows = call(pack_kernel, (shape((PACKED, 128), bf16), shape((8, 72, 128), bf16)))(coef)
    line = lax.all_gather(packed, "pair", axis_index_groups=FAR, tiled=True)
    line = lax.all_gather(line, "pair", axis_index_groups=NEAR, tiled=True)
    line, rows = lax.optimization_barrier((line, rows))
    column = lax.ppermute(line, "pair", swap(2))
    rows = lax.all_to_all(rows, ("pair", "spin"), 0, 0, axis_index_groups=ROWS)
    line, column, rows = lax.optimization_barrier((line, column, rows))
    far_rows = lax.ppermute(rows, "spin", swap(1, SPIN))

    own = jnp.concatenate([line, column])
    other = lax.ppermute(own, "pair", swap(1))
    half = call(
        half_kernel,
        shape((PQ * K, 4 * S), bf16),
        [pl.BlockSpec(memory_space=pltpu.SMEM), vmem, vmem, pl.BlockSpec((PQ, S, PLANES * PLANE // 2), lambda i: (0, 0, i))],
        50,
        grid=(2,),
        scratch_shapes=[pltpu.VMEM((CK, PQ * S), jnp.float32)],
    )(live, own.reshape(2, PLANES, PACKED, 128), other.reshape(2, PLANES, PACKED, 128), integrals)
    halves = lax.all_gather(half, "pair", axis_index_groups=CHIP)
    sign = jnp.asarray(signs(), bf16)
    keep, give = call(term_kernel, (shape((SPIN, 72, 128), jnp.float32), shape((SPIN, 72, 128), bf16)))(
        halves, rows, far_rows, sign
    )
    given = lax.all_gather(give, "pair", axis_index_groups=ACROSS)
    terms = call(join_kernel, shape((PLANES, 40, 128), bf16))(keep, given)
    terms = lax.all_to_all(terms, "pair", 0, 0, axis_index_groups=LINE)
    sums = call(sum_kernel, shape((40, 128), jnp.float32))(terms)
    sums = lax.all_gather(sums, "pair", axis_index_groups=PLANE_PAIRS)
    out = call(result_kernel, shape((2, J, PQ, 2 * K), jnp.float32))(sums)
    return out.transpose(0, 2, 3, 1)


def solution(mesh):
    placed = (P(None, "pair", None), P(None, "pair", "spin"), P())
    return jax.shard_map(
        shards, mesh=mesh, in_specs=placed, out_specs=P(None, None, "spin", "pair"), check_vma=False
    )
```

```python
import jax
import jax.numpy as jnp
import numpy as np
from jax import lax
from jax.experimental import pallas as pl
from jax.experimental.pallas import tpu as pltpu
from jax.sharding import PartitionSpec as P

S, K, PQ, PLANES, Q, SPIN = 96, 48, 4, 16, 4, 8
J = K // Q
PLANE = Q * S
CK = 4 * K
PACKED = CK * S // 128

FOLD = [0, 1, 3, 2]
NEAR = [[4 * (4 * h + l) + q for l in FOLD] for h in range(4) for q in range(Q)]
FAR = [[4 * (4 * h + l) + q for h in range(4)] for l in range(4) for q in range(Q)]
LINE = [[4 * z + q for z in range(PLANES)] for q in range(Q)]
CHIP = [[2 * i, 2 * i + 1] for i in range(Q * PLANES // 2)]
PLANE_PAIRS = [[8 * z + q, 8 * z + 4 + q] for z in range(PLANES // 2) for q in range(Q)]
ACROSS = [[4 * z + c, 4 * z + 2 + c] for z in range(PLANES) for c in range(2)]
ROWS = [[SPIN * (2 * i + c) + 2 * y + x for c in range(2) for y in range(4)] for i in range(Q * PLANES // 2) for x in range(2)]


def swap(bit, size=Q * PLANES):
    return [(i, i ^ bit) for i in range(size)]


def signs():
    table = (
        ((0, 1), (1, 1), (2, 1), (3, 1)),
        ((1, 1), (0, -1), (3, 1), (2, -1)),
        ((2, -1), (3, 1), (0, 1), (1, -1)),
        ((3, 1), (2, 1), (1, -1), (0, -1)),
    )
    out = np.zeros((4, 4, J, 4, J), np.float32)
    for v, row in enumerate(table):
        for c, (source, sign) in enumerate(row):
            for j in range(J):
                out[c, v, j, source, j] = sign
    return np.kron(np.eye(2, dtype=np.float32), out.reshape(CK, 4 * J))


def nt(a, b):
    return lax.dot_general(a, b, (((1,), (1,)), ((), ())), preferred_element_type=jnp.float32)


def turn(x, lanes):
    return x if lanes == 0 else jnp.concatenate([x[:, 128 - lanes :], x[:, : 128 - lanes]], axis=1)


def pack_kernel(coef_ref, out_ref, rows_ref):
    q = lax.axis_index("pair") % Q
    full = coef_ref[...].reshape(CK, S)
    tail = full[PACKED:]
    side = jnp.concatenate([tail[:, 32 * i : 32 * i + 32] for i in range(3)], axis=0)
    packed = jnp.concatenate([full[:PACKED], side], axis=1)
    turned = packed
    for place in range(1, Q):
        turned = jnp.where(q == place, turn(packed, S * place % 128), turned)
    out_ref[...] = turned
    row = lax.broadcasted_iota(jnp.int32, (CK, CK), 0)
    core = (row >= 8 * J).astype(jnp.int32)
    row = row - 8 * J * core
    x = (row >= 4 * J).astype(jnp.int32)
    row = row - 4 * J * x
    component = sum((row >= J * c).astype(jnp.int32) for c in range(1, 4))
    wanted = (K - J) * component + row + J * (2 * x + core)
    pick = (lax.broadcasted_iota(jnp.int32, (CK, CK), 1) == wanted).astype(jnp.bfloat16)
    rows = jnp.dot(pick, full, preferred_element_type=jnp.float32)
    for core in range(2):
        first, second = (rows[4 * J * i : 4 * J * (i + 1)] for i in (2 * core, 2 * core + 1))
        top = jnp.concatenate([first, second[:, :32]], axis=1)
        low = jnp.concatenate([second[: 2 * J, 32:], second[2 * J :, 32:]], axis=1)
        block = jnp.concatenate([top, low], axis=0).astype(jnp.bfloat16)
        for y in range(4):
            rows_ref[4 * core + y] = block


def plane_of(blocks, lane):
    p0, p1, p2, p3 = blocks
    main = [jnp.where(lane < 96, p0, p1), jnp.where(lane < 64, p1, p2), jnp.where(lane < 32, p2, p3)]
    side = jnp.where(lane < 32, p3, jnp.where(lane < 64, p2, jnp.where(lane < 96, p1, p0)))
    turned = [turn(side[K * i : K * i + K], 32 * (i + 1)) for i in range(3)]
    low = lane[:K]
    tail = [
        jnp.where((low >= 32) & (low < 64), turned[(t + 1) % 3], jnp.where((low >= 64) & (low < 96), turned[(t + 2) % 3], turned[t]))
        for t in range(3)
    ]
    return jnp.concatenate([jnp.concatenate(main, axis=1), jnp.concatenate(tail, axis=1)], axis=0)


def half_kernel(live_ref, own_ref, other_ref, integrals_ref, half_ref, total_ref):
    step = pl.program_id(0)
    here = lax.axis_index("pair")
    x, core = here % Q // 2, here % 2
    lane = lax.broadcasted_iota(jnp.int32, (PACKED, 128), 1)
    planes = []
    for i in range(PLANES // 2):
        slot = FOLD.index(i % 4) * 4 + 2 * step + i // 4
        blocks = []
        for place in range(Q):
            column = (place // 2) ^ x
            blocks.append(jnp.where(core == place % 2, own_ref[column, slot], other_ref[column, slot]))
        planes.append(plane_of(blocks, lane))
    term = nt(jnp.concatenate(planes, axis=1), integrals_ref[...].reshape(PQ * S, PLANES * PLANE // 2))

    @pl.when(step == 0)
    def _():
        total_ref[...] = term

    @pl.when(step == 1)
    def _():
        total = total_ref[...] + term
        keep = lax.broadcasted_iota(jnp.int32, (CK, S), 1) < live_ref[here]
        for pq in range(PQ):
            part = jnp.where(keep, total[:, pq * S : (pq + 1) * S], 0.0)
            row = jnp.concatenate([part[c * K : (c + 1) * K] for c in range(4)], axis=1)
            half_ref[pq * K : (pq + 1) * K, :] = row.astype(jnp.bfloat16)


def rows_of(block):
    block = block.astype(jnp.float32)
    low = jnp.concatenate([block[4 * J :, :64], block[4 * J :, 64:]], axis=0)
    return jnp.concatenate([block[: 4 * J, :S], jnp.concatenate([block[: 4 * J, S:], low], axis=1)], axis=0)


def weights_of(rows_ref, y, signs_ref):
    rows = jnp.concatenate([rows_of(rows_ref[4 * core + y]) for core in range(2)], axis=1).astype(jnp.bfloat16)
    return jnp.dot(signs_ref[...], rows, preferred_element_type=jnp.float32).astype(jnp.bfloat16)


def term_kernel(half_ref, rows_ref, far_rows_ref, signs_ref, keep_ref, give_ref):
    x = lax.axis_index("pair") % Q // 2
    side = lax.axis_index("spin") % 2
    half = [jnp.concatenate([half_ref[core, :, c * S : (c + 1) * S] for core in range(2)], axis=1) for c in range(4)]
    signed = [weights_of(ref, y, signs_ref) for ref in (rows_ref, far_rows_ref) for y in range(4)]
    terms = []
    for column in range(2):
        term = None
        for c in range(4):
            at = 4 * J * (4 * column + c)
            more = nt(jnp.concatenate([part[at : at + 4 * J] for part in signed], axis=0), half[c])
            term = more if term is None else term + more
        terms.append(term)
    for term, ref in ((jnp.where(x == 0, terms[0], terms[1]), keep_ref), (jnp.where(x == 0, terms[1], terms[0]), give_ref)):
        for e in range(SPIN):
            part = term[e * 4 * J : (e + 1) * 4 * J]
            tail = jnp.concatenate([part[: 2 * J, 128:], part[2 * J :, 128:]], axis=1)
            block = 2 * (e % 4) + (side if e < 4 else 1 - side)
            ref[block] = jnp.concatenate([part[:, :128], tail], axis=0).astype(ref.dtype)


def join_kernel(keep_ref, given_ref, out_ref):
    partner = 1 - lax.axis_index("pair") % Q // 2
    for e in range(SPIN):
        block = keep_ref[e] + given_ref[partner, e].astype(jnp.float32)
        out_ref[2 * e] = block[:40].astype(jnp.bfloat16)
        out_ref[2 * e + 1] = block[32:].astype(jnp.bfloat16)


def sum_kernel(terms_ref, out_ref):
    total = terms_ref[0].astype(jnp.float32)
    for z in range(1, PLANES):
        total = total + terms_ref[z].astype(jnp.float32)
    out_ref[...] = total


def result_kernel(sums_ref, out_ref):
    total = jnp.concatenate([sums_ref[0], sums_ref[1, 8:]], axis=0)
    side = total[4 * J :]
    full = jnp.concatenate([total[: 4 * J], jnp.concatenate([side[:, :64], side[:, 64:]], axis=0)], axis=1)
    real, imag, real_bar, imag_bar = (full[v * J : (v + 1) * J] for v in range(4))
    barred = (lax.axis_index("pair") // Q) % 2 == 1
    parts = (
        (jnp.where(barred, real_bar, real), jnp.where(barred, real, -real_bar)),
        (jnp.where(barred, imag_bar, imag), jnp.where(barred, -imag, imag_bar)),
    )
    for t, (unbarred, partner) in enumerate(parts):
        for pq in range(PQ):
            columns = slice(pq * K, (pq + 1) * K)
            out_ref[t, :, pq, :] = jnp.concatenate([unbarred[:, columns], partner[:, columns]], axis=1)


def call(kernel, out_shape, in_specs=None, mib=16, **more):
    vmem = pl.BlockSpec(memory_space=pltpu.VMEM)

    def run(*args):
        return pl.pallas_call(
            kernel,
            out_shape=out_shape,
            in_specs=in_specs or [vmem] * len(args),
            out_specs=jax.tree.map(lambda _: vmem, out_shape),
            compiler_params=pltpu.CompilerParams(vmem_limit_bytes=mib * 1024 * 1024),
            **more,
        )(*args)

    return run


def shards(integrals, coef, live):
    bf16 = jnp.bfloat16
    shape = jax.ShapeDtypeStruct
    vmem = pl.BlockSpec(memory_space=pltpu.VMEM)
    coef = coef.transpose(0, 2, 1)
    packed, rows = call(pack_kernel, (shape((PACKED, 128), bf16), shape((8, 72, 128), bf16)))(coef)
    line = lax.all_gather(packed, "pair", axis_index_groups=FAR, tiled=True)
    line = lax.all_gather(line, "pair", axis_index_groups=NEAR, tiled=True)
    line, rows = lax.optimization_barrier((line, rows))
    column = lax.ppermute(line, "pair", swap(2))
    rows = lax.all_to_all(rows, ("pair", "spin"), 0, 0, axis_index_groups=ROWS)
    line, column, rows = lax.optimization_barrier((line, column, rows))
    far_rows = lax.ppermute(rows, "spin", swap(1, SPIN))

    own = jnp.concatenate([line, column])
    other = lax.ppermute(own, "pair", swap(1))
    half = call(
        half_kernel,
        shape((PQ * K, 4 * S), bf16),
        [pl.BlockSpec(memory_space=pltpu.SMEM), vmem, vmem, pl.BlockSpec((PQ, S, PLANES * PLANE // 2), lambda i: (0, 0, i))],
        50,
        grid=(2,),
        scratch_shapes=[pltpu.VMEM((CK, PQ * S), jnp.float32)],
    )(live, own.reshape(2, PLANES, PACKED, 128), other.reshape(2, PLANES, PACKED, 128), integrals)
    halves = lax.all_gather(half, "pair", axis_index_groups=CHIP)
    sign = jnp.asarray(signs(), bf16)
    keep, give = call(term_kernel, (shape((SPIN, 72, 128), jnp.float32), shape((SPIN, 72, 128), bf16)))(
        halves, rows, far_rows, sign
    )
    given = lax.all_gather(give, "pair", axis_index_groups=ACROSS)
    terms = call(join_kernel, shape((PLANES, 40, 128), bf16))(keep, given)
    terms = lax.all_to_all(terms, "pair", 0, 0, axis_index_groups=LINE)
    sums = call(sum_kernel, shape((40, 128), jnp.float32))(terms)
    sums = lax.all_gather(sums, "pair", axis_index_groups=PLANE_PAIRS)
    out = call(result_kernel, shape((2, J, PQ, 2 * K), jnp.float32))(sums)
    return out.transpose(0, 2, 3, 1)


def solution(mesh):
    placed = (P(None, "pair", None), P(None, "pair", "spin"), P())
    return jax.shard_map(
        shards, mesh=mesh, in_specs=placed, out_specs=P(None, None, "spin", "pair"), check_vma=False
    )
```

```python
import jax
import jax.numpy as jnp
import numpy as np
from jax import lax
from jax.experimental import pallas as pl
from jax.experimental.pallas import tpu as pltpu
from jax.sharding import PartitionSpec as P

S, K, PQ, PLANES, Q, SPIN = 96, 48, 4, 16, 4, 8
J = K // Q
PLANE = Q * S
CK = 4 * K
PACKED = CK * S // 128

FOLD = [0, 1, 3, 2]
NEAR = [[4 * (4 * h + l) + q for l in FOLD] for h in range(4) for q in range(Q)]
FAR = [[4 * (4 * h + l) + q for h in range(4)] for l in range(4) for q in range(Q)]
LINE = [[4 * z + q for z in range(PLANES)] for q in range(Q)]
CHIP = [[2 * i, 2 * i + 1] for i in range(Q * PLANES // 2)]
PLANE_PAIRS = [[8 * z + q, 8 * z + 4 + q] for z in range(PLANES // 2) for q in range(Q)]
ACROSS = [[4 * z + c, 4 * z + 2 + c] for z in range(PLANES) for c in range(2)]
ROWS = [[SPIN * (2 * i + c) + 2 * y + x for c in range(2) for y in range(4)] for i in range(Q * PLANES // 2) for x in range(2)]


def swap(bit, size=Q * PLANES):
    return [(i, i ^ bit) for i in range(size)]


def signs():
    table = (
        ((0, 1), (1, 1), (2, 1), (3, 1)),
        ((1, 1), (0, -1), (3, 1), (2, -1)),
        ((2, -1), (3, 1), (0, 1), (1, -1)),
        ((3, 1), (2, 1), (1, -1), (0, -1)),
    )
    out = np.zeros((4, 4, J, 4, J), np.float32)
    for v, row in enumerate(table):
        for c, (source, sign) in enumerate(row):
            for j in range(J):
                out[c, v, j, source, j] = sign
    return np.kron(np.eye(2, dtype=np.float32), out.reshape(CK, 4 * J))


def nt(a, b):
    return lax.dot_general(a, b, (((1,), (1,)), ((), ())), preferred_element_type=jnp.float32)


def turn(x, lanes):
    return x if lanes == 0 else jnp.concatenate([x[:, 128 - lanes :], x[:, : 128 - lanes]], axis=1)


def pack_kernel(coef_ref, out_ref, rows_ref):
    q = lax.axis_index("pair") % Q
    full = coef_ref[...].reshape(CK, S)
    tail = full[PACKED:]
    side = jnp.concatenate([tail[:, 32 * i : 32 * i + 32] for i in range(3)], axis=0)
    packed = jnp.concatenate([full[:PACKED], side], axis=1)
    turned = packed
    for place in range(1, Q):
        turned = jnp.where(q == place, turn(packed, S * place % 128), turned)
    out_ref[...] = turned
    row = lax.broadcasted_iota(jnp.int32, (CK, CK), 0)
    core = (row >= 8 * J).astype(jnp.int32)
    row = row - 8 * J * core
    x = (row >= 4 * J).astype(jnp.int32)
    row = row - 4 * J * x
    component = sum((row >= J * c).astype(jnp.int32) for c in range(1, 4))
    wanted = (K - J) * component + row + J * (2 * x + core)
    pick = (lax.broadcasted_iota(jnp.int32, (CK, CK), 1) == wanted).astype(jnp.bfloat16)
    rows = jnp.dot(pick, full, preferred_element_type=jnp.float32)
    for core in range(2):
        first, second = (rows[4 * J * i : 4 * J * (i + 1)] for i in (2 * core, 2 * core + 1))
        top = jnp.concatenate([first, second[:, :32]], axis=1)
        low = jnp.concatenate([second[: 2 * J, 32:], second[2 * J :, 32:]], axis=1)
        block = jnp.concatenate([top, low], axis=0).astype(jnp.bfloat16)
        for y in range(4):
            rows_ref[4 * core + y] = block


def plane_of(blocks, lane):
    p0, p1, p2, p3 = blocks
    main = [jnp.where(lane < 96, p0, p1), jnp.where(lane < 64, p1, p2), jnp.where(lane < 32, p2, p3)]
    side = jnp.where(lane < 32, p3, jnp.where(lane < 64, p2, jnp.where(lane < 96, p1, p0)))
    turned = [turn(side[K * i : K * i + K], 32 * (i + 1)) for i in range(3)]
    low = lane[:K]
    tail = [
        jnp.where((low >= 32) & (low < 64), turned[(t + 1) % 3], jnp.where((low >= 64) & (low < 96), turned[(t + 2) % 3], turned[t]))
        for t in range(3)
    ]
    return jnp.concatenate([jnp.concatenate(main, axis=1), jnp.concatenate(tail, axis=1)], axis=0)


def half_kernel(live_ref, own_ref, other_ref, integrals_ref, half_ref, total_ref):
    step = pl.program_id(0)
    here = lax.axis_index("pair")
    x, core = here % Q // 2, here % 2
    lane = lax.broadcasted_iota(jnp.int32, (PACKED, 128), 1)
    planes = []
    for i in range(PLANES // 2):
        slot = FOLD.index(i % 4) * 4 + 2 * step + i // 4
        blocks = []
        for place in range(Q):
            column = (place // 2) ^ x
            blocks.append(jnp.where(core == place % 2, own_ref[column, slot], other_ref[column, slot]))
        planes.append(plane_of(blocks, lane))
    term = nt(jnp.concatenate(planes, axis=1), integrals_ref[...].reshape(PQ * S, PLANES * PLANE // 2))

    @pl.when(step == 0)
    def _():
        total_ref[...] = term

    @pl.when(step == 1)
    def _():
        total = total_ref[...] + term
        keep = lax.broadcasted_iota(jnp.int32, (CK, S), 1) < live_ref[here]
        for pq in range(PQ):
            part = jnp.where(keep, total[:, pq * S : (pq + 1) * S], 0.0)
            row = jnp.concatenate([part[c * K : (c + 1) * K] for c in range(4)], axis=1)
            half_ref[pq * K : (pq + 1) * K, :] = row.astype(jnp.bfloat16)


def rows_of(block):
    block = block.astype(jnp.float32)
    low = jnp.concatenate([block[4 * J :, :64], block[4 * J :, 64:]], axis=0)
    return jnp.concatenate([block[: 4 * J, :S], jnp.concatenate([block[: 4 * J, S:], low], axis=1)], axis=0)


def weights_of(rows_ref, y, signs_ref):
    rows = jnp.concatenate([rows_of(rows_ref[4 * core + y]) for core in range(2)], axis=1).astype(jnp.bfloat16)
    return jnp.dot(signs_ref[...], rows, preferred_element_type=jnp.float32).astype(jnp.bfloat16)


def term_kernel(half_ref, rows_ref, far_rows_ref, signs_ref, keep_ref, give_ref):
    x = lax.axis_index("pair") % Q // 2
    side = lax.axis_index("spin") % 2
    half = [jnp.concatenate([half_ref[core, :, c * S : (c + 1) * S] for core in range(2)], axis=1) for c in range(4)]
    signed = [weights_of(ref, y, signs_ref) for ref in (rows_ref, far_rows_ref) for y in range(4)]
    terms = []
    for column in range(2):
        term = None
        for c in range(4):
            at = 4 * J * (4 * column + c)
            more = nt(jnp.concatenate([part[at : at + 4 * J] for part in signed], axis=0), half[c])
            term = more if term is None else term + more
        terms.append(term)
    for term, ref in ((jnp.where(x == 0, terms[0], terms[1]), keep_ref), (jnp.where(x == 0, terms[1], terms[0]), give_ref)):
        for e in range(SPIN):
            part = term[e * 4 * J : (e + 1) * 4 * J]
            tail = jnp.concatenate([part[: 2 * J, 128:], part[2 * J :, 128:]], axis=1)
            block = 2 * (e % 4) + (side if e < 4 else 1 - side)
            ref[block] = jnp.concatenate([part[:, :128], tail], axis=0).astype(ref.dtype)


def join_kernel(keep_ref, given_ref, out_ref):
    partner = 1 - lax.axis_index("pair") % Q // 2
    for e in range(SPIN):
        block = keep_ref[e] + given_ref[partner, e].astype(jnp.float32)
        out_ref[2 * e] = block[:40].astype(jnp.bfloat16)
        out_ref[2 * e + 1] = block[32:].astype(jnp.bfloat16)


def sum_kernel(terms_ref, out_ref):
    total = terms_ref[0].astype(jnp.float32)
    for z in range(1, PLANES):
        total = total + terms_ref[z].astype(jnp.float32)
    out_ref[...] = total


def result_kernel(sums_ref, out_ref):
    total = jnp.concatenate([sums_ref[0], sums_ref[1, 8:]], axis=0)
    side = total[4 * J :]
    full = jnp.concatenate([total[: 4 * J], jnp.concatenate([side[:, :64], side[:, 64:]], axis=0)], axis=1)
    real, imag, real_bar, imag_bar = (full[v * J : (v + 1) * J] for v in range(4))
    barred = (lax.axis_index("pair") // Q) % 2 == 1
    parts = (
        (jnp.where(barred, real_bar, real), jnp.where(barred, real, -real_bar)),
        (jnp.where(barred, imag_bar, imag), jnp.where(barred, -imag, imag_bar)),
    )
    for t, (unbarred, partner) in enumerate(parts):
        for pq in range(PQ):
            columns = slice(pq * K, (pq + 1) * K)
            out_ref[t, :, pq, :] = jnp.concatenate([unbarred[:, columns], partner[:, columns]], axis=1)


def call(kernel, out_shape, in_specs=None, mib=16, **more):
    vmem = pl.BlockSpec(memory_space=pltpu.VMEM)

    def run(*args):
        return pl.pallas_call(
            kernel,
            out_shape=out_shape,
            in_specs=in_specs or [vmem] * len(args),
            out_specs=jax.tree.map(lambda _: vmem, out_shape),
            compiler_params=pltpu.CompilerParams(vmem_limit_bytes=mib * 1024 * 1024),
            **more,
        )(*args)

    return run


def shards(integrals, coef, live):
    bf16 = jnp.bfloat16
    shape = jax.ShapeDtypeStruct
    vmem = pl.BlockSpec(memory_space=pltpu.VMEM)
    coef = coef.transpose(0, 2, 1)
    packed, rows = call(pack_kernel, (shape((PACKED, 128), bf16), shape((8, 72, 128), bf16)))(coef)
    line = lax.all_gather(packed, "pair", axis_index_groups=FAR, tiled=True)
    line = lax.all_gather(line, "pair", axis_index_groups=NEAR, tiled=True)
    line, rows = lax.optimization_barrier((line, rows))
    column = lax.ppermute(line, "pair", swap(2))
    rows = lax.all_to_all(rows, ("pair", "spin"), 0, 0, axis_index_groups=ROWS)
    line, column, rows = lax.optimization_barrier((line, column, rows))
    far_rows = lax.ppermute(rows, "spin", swap(1, SPIN))

    own = jnp.concatenate([line, column])
    other = lax.ppermute(own, "pair", swap(1))
    half = call(
        half_kernel,
        shape((PQ * K, 4 * S), bf16),
        [pl.BlockSpec(memory_space=pltpu.SMEM), vmem, vmem, pl.BlockSpec((PQ, S, PLANES * PLANE // 2), lambda i: (0, 0, i))],
        24,
        grid=(2,),
        scratch_shapes=[pltpu.VMEM((CK, PQ * S), jnp.float32)],
    )(live, own.reshape(2, PLANES, PACKED, 128), other.reshape(2, PLANES, PACKED, 128), integrals)
    halves = lax.all_gather(half, "pair", axis_index_groups=CHIP)
    sign = jnp.asarray(signs(), bf16)
    keep, give = call(term_kernel, (shape((SPIN, 72, 128), jnp.float32), shape((SPIN, 72, 128), bf16)))(
        halves, rows, far_rows, sign
    )
    given = lax.all_gather(give, "pair", axis_index_groups=ACROSS)
    terms = call(join_kernel, shape((PLANES, 40, 128), bf16))(keep, given)
    terms = lax.all_to_all(terms, "pair", 0, 0, axis_index_groups=LINE)
    sums = call(sum_kernel, shape((40, 128), jnp.float32))(terms)
    sums = lax.all_gather(sums, "pair", axis_index_groups=PLANE_PAIRS)
    out = call(result_kernel, shape((2, J, PQ, 2 * K), jnp.float32))(sums)
    return out.transpose(0, 2, 3, 1)


def solution(mesh):
    placed = (P(None, "pair", None), P(None, "pair", "spin"), P())
    return jax.shard_map(
        shards, mesh=mesh, in_specs=placed, out_specs=P(None, None, "spin", "pair"), check_vma=False
    )
```
